32 devices in a mesh: blk: 8 (over y, x, core), sub: 4 (over z).
Axes of the slice: x: 2, y: 2, z: 4, core: 2. Of those that a mesh axis runs over, the one named last changes fastest.
Arguments:
- user_factors: float32 [32768, 1024], P(('blk', 'sub')), may hold values from -6 to 6
- item_factors: bfloat16 [2048, 1024], P(('blk', 'sub')), may hold values from -6 to 6
- ratings: bfloat16 [32768, 1024], P(('blk', 'sub')), may hold values from -6 to 6
- presence: int32 [256, 8, 2], P(('blk', 'sub')), may hold values 0 or 1
- visit_order: int32 [8], replicated, may hold values from 0 to 7, each once
Outputs:
- users_out: float32 [32768, 1024], P(('blk', 'sub'))
- items_out: bfloat16 [2048, 1024], P(('blk', 'sub'))
The draws below stay inside these ranges and needn't reach their ends.
All inputs are finite; a program needn't handle non-finite values. No bound on the sum of `presence` on one device may be relied on, other than what follows from the above.
Results may differ from the reference program's by a relative error of at most 0.017.
Values may be sent and summed in bfloat16 or wider, within the bound.
A program may use at most 64 MiB of HBM per device.

```python
import math
import jax
import jax.numpy as jnp
from jax import lax

R = 1024
BS = 256
TILE = 128
TICKS = 4
U_DEV = 1024
USERS = 32768
ITEMS = 2048
N_BLK = 8
N_SUB = 4


def draw_user_factors(key, part):
    inner = jax.random.fold_in(key, 11)
    values = jnp.clip(jax.random.normal(inner, (USERS, R), jnp.float32), -6.0, 6.0)
    return values


def draw_item_factors(key, part):
    inner = jax.random.fold_in(key, 23)
    values = jnp.clip(jax.random.normal(inner, (ITEMS, R), jnp.float32), -6.0, 6.0)
    return values.astype(jnp.bfloat16)


def place_ends(values, stream_key, smallest, high):
    shape = values.shape
    index_at = [jax.random.randint(jax.random.fold_in(stream_key, axis), (), 0, shape[axis]) for axis in range(len(shape))]
    values = values.at[tuple(index_at)].set(smallest)
    longest = shape.index(max(shape))
    index_at[longest] = (index_at[longest] + 1) % shape[longest]
    return values.at[tuple(index_at)].set(high)


def block_scale(rng, dims, pieces, smallest, high):
    level = 1.0
    for axis_at, blocks in pieces:
        draws = jax.random.uniform(jax.random.fold_in(jax.random.fold_in(rng, 6), axis_at), (blocks,), jnp.float32, smallest / len(pieces), high / len(pieces))
        level = level * jnp.repeat(jnp.exp(draws), dims[axis_at] // blocks).reshape((-1,) + (1,) * (len(dims) - 1 - axis_at))
    return level


def bell_draw(rng, dims, spread, limit, cuts=(), held_as=jnp.bfloat16):
    array = spread * jax.random.normal(rng, dims, jnp.float32)
    if cuts:
        array = array * block_scale(rng, dims, cuts, -0.22, 0.18)
    return jnp.clip(array, -limit, limit).astype(held_as)


def setup_inputs(seed: int = 0) -> dict:
    key_of = jax.random.split(jax.random.key(seed), 6)
    return {
        "user_factors": draw_user_factors(jax.random.fold_in(key_of[5], 71), 0),
        "item_factors": draw_item_factors(jax.random.fold_in(key_of[5], 71), 0),
        "ratings": bell_draw(key_of[2], (USERS, TICKS * BS), 1.0, 6.0, ((0, 32),)),
        "presence": place_ends((jax.random.randint(key_of[3], (USERS // TILE, N_BLK, BS // TILE), 0, 2) < 1).astype(jnp.int32), jax.random.fold_in(key_of[3], 1), 0, 1),
        "visit_order": jax.random.permutation(key_of[4], N_BLK).astype(jnp.int32),
    }


learn_users = 0.5
decay_weight = 0.05

def reference(user_factors, item_factors, ratings, presence, visit_order):
    scale = R ** (-0.5)
    step_items = 0.9 * R / (math.sqrt(N_SUB * U_DEV) + math.sqrt(R)) ** 2
    tile_users = U_DEV // TILE
    tile_items = BS // TILE
    held = item_factors.reshape(N_BLK, BS, R)
    grouped = user_factors.reshape(N_BLK, N_SUB, U_DEV, R)
    pres_grouped = presence.reshape(N_BLK, N_SUB, tile_users, N_BLK, tile_items)
    rate_grouped = ratings.reshape(N_BLK, N_SUB, U_DEV, TICKS, BS)
    for step_index in range(TICKS):
        idents = jnp.roll(visit_order, step_index).astype(jnp.int32)

        def visit(packed):
            users_now, block_now, pres_now, rate_now, ident = packed
            picked = jnp.take(pres_now, ident, axis=2)
            present = jnp.broadcast_to(picked[:, :, None, :, None], (N_SUB, tile_users, TILE, tile_items, TILE))
            present = present.reshape(N_SUB, U_DEV, BS).astype(jnp.float32)
            users_half = users_now.astype(jnp.bfloat16).astype(jnp.float32)
            block_wide = block_now.astype(jnp.float32)
            predicted = jnp.einsum('sur,ir->sui', users_half, block_wide) * scale
            residual = (present * (predicted - rate_now.astype(jnp.float32))).astype(jnp.bfloat16).astype(jnp.float32)
            user_grad = jnp.einsum('sui,ir->sur', residual, block_wide) * scale
            item_part = (jnp.einsum('sui,sur->sir', residual, users_half) * scale).astype(jnp.bfloat16)
            item_grad = lax.optimization_barrier(jnp.sum(item_part.astype(jnp.float32), axis=0))
            users_next = users_now - learn_users * (user_grad + decay_weight * users_now)
            block_next = (block_wide - step_items * (item_grad + decay_weight * block_wide)).astype(jnp.bfloat16)
            return (users_next, block_next)
        grouped, updated = lax.map(visit, (grouped, held, pres_grouped, rate_grouped[:, :, :, step_index], idents))
        held = jnp.roll(updated, 1, axis=0)
    return (grouped.reshape(USERS, R), held.reshape(ITEMS, R))
```

```python
import functools
import math

import jax
import jax.numpy as jnp
from jax import lax
from jax.experimental import pallas as pl
from jax.experimental.pallas import tpu as pltpu
from jax.sharding import PartitionSpec as P

R = 1024
BS = 256
TICKS = 4
MESH = pl.DeviceIdType.MESH

learn_users = 0.5
decay_weight = 0.05


def passed_along(block, axis, distance):
    devices = range(lax.axis_size(axis))
    route = [((i - distance) % len(devices), i) for i in devices]
    return lax.ppermute(block, axis, route)


def step_size(group_users):
    return 0.9 * R / (math.sqrt(group_users) + math.sqrt(R)) ** 2


def by_collectives(user_factors, item_factors, ratings, presence, visit_order):
    scale = R ** (-0.5)
    group_count = lax.axis_size("blk")
    group = lax.axis_index("blk")
    part_index = lax.axis_index("sub")
    part_rows = item_factors.shape[0]
    local_users = user_factors.shape[0]
    step_items = step_size(lax.axis_size("sub") * local_users)
    tile_users = presence.shape[0]
    tile_items = presence.shape[2]
    users_now = user_factors
    held_part = item_factors
    for step_index in range(TICKS):
        item_block = lax.all_gather(held_part, "sub", axis=0, tiled=True)
        position = jnp.mod(group - step_index, group_count)
        ident = jnp.sum(jnp.where(jnp.arange(group_count) == position, visit_order, 0))
        picked = lax.dynamic_index_in_dim(presence, ident, 1, keepdims=False)
        present = jnp.broadcast_to(
            picked[:, None, :, None],
            (tile_users, local_users // tile_users, tile_items, BS // tile_items),
        )
        present = present.reshape(local_users, BS).astype(jnp.float32)
        users_half = users_now.astype(jnp.bfloat16)
        predicted = (
            lax.dot_general(
                users_half, item_block, (((1,), (1,)), ((), ())), preferred_element_type=jnp.float32
            )
            * scale
        )
        targets = ratings[:, step_index * BS : (step_index + 1) * BS].astype(jnp.float32)
        residual = (present * (predicted - targets)).astype(jnp.bfloat16)
        user_grad = jnp.dot(residual, item_block, preferred_element_type=jnp.float32) * scale
        item_part = (
            lax.dot_general(
                residual, users_half, (((0,), (0,)), ((), ())), preferred_element_type=jnp.float32
            )
            * scale
        ).astype(jnp.bfloat16)
        users_now = users_now - learn_users * (user_grad + decay_weight * users_now)
        item_grad = lax.psum_scatter(item_part, "sub", scatter_dimension=0, tiled=True).astype(
            jnp.float32
        )
        own_rows = lax.dynamic_slice_in_dim(
            item_block, part_index * part_rows, part_rows, 0
        ).astype(jnp.float32)
        updated = (own_rows - step_items * (item_grad + decay_weight * own_rows)).astype(
            jnp.bfloat16
        )
        held_part = passed_along(updated, "blk", 1)
    return (users_now, held_part)


LINE = 4
CHUNKS = 2
HALVES = 2


def line_kernel(
    n_blk, step_items,
    users_hbm, items_hbm, ratings_hbm, presence_ref, order_ref,
    users_out, items_out,
    users, items, users_half, ratings, targets, res, res_t, first_sum, blk, part, sent, upd, final,
    local_sem, gather_send, gather_recv, part_send, part_recv,
    final_send, final_recv,
):
    scale = R ** (-0.5)
    g, s = lax.axis_index("blk"), lax.axis_index("sub")
    onward, back = lax.rem(g + 1, n_blk), lax.rem(g + n_blk - 1, n_blk)
    n_users = users.shape[0]
    rows = items.shape[0] // CHUNKS
    size = LINE * rows
    wide = R // HALVES
    tile_users, tile_items = presence_ref.shape[0], presence_ref.shape[1]
    tile_rows = n_users // tile_users

    def remote(src, dst, send, recv, device):
        return pltpu.make_async_remote_copy(
            src_ref=src, dst_ref=dst, send_sem=send, recv_sem=recv,
            device_id=device, device_id_type=MESH,
        )

    def some(first, count=1):
        return pl.ds(pl.multiple_of(first * rows, rows), count * rows)

    def columns(h):
        return pl.ds(h * wide, wide)

    load_items = pltpu.make_async_copy(items_hbm, items, local_sem.at[0])
    load_users = pltpu.make_async_copy(users_hbm, users, local_sem.at[1])
    load_ratings = pltpu.make_async_copy(ratings_hbm, ratings, local_sem.at[2])
    load_items.start()
    load_users.start()
    load_ratings.start()

    barrier = pltpu.get_barrier_semaphore()
    for k in range(1, LINE):
        pl.semaphore_signal(
            barrier, inc=1, device_id=(g, lax.rem(s + k, LINE)), device_id_type=MESH
        )
    for group in (onward, back):
        for k in range(LINE):
            pl.semaphore_signal(barrier, inc=1, device_id=(group, k), device_id_type=MESH)
    pl.semaphore_wait(barrier, 3 * LINE - 1)

    def chunk_rows(c, j, count=1):
        return pl.ds(pl.multiple_of(c * size + j * rows, rows), count * rows)

    def first_copies(c, h):
        src = items.at[pl.ds(c * rows, rows), columns(h)]
        return [
            remote(src, blk.at[0, chunk_rows(c, s), columns(h)], gather_send.at[0, c, h, k],
                   gather_recv.at[0, c, h], (g, lax.rem(s + 1 + k, LINE)))
            for k in range(LINE - 1)
        ]

    def gather_copies(t, c, h):
        return [
            remote(upd.at[t, c, h], blk.at[t + 1, chunk_rows(c, s), columns(h)],
                   gather_send.at[t + 1, c, h, k], gather_recv.at[t + 1, c, h],
                   (onward, lax.rem(s + k, LINE)))
            for k in range(LINE)
        ]

    def arrival(t, c, h):
        count = LINE - 1 if t == 0 else LINE
        ref = blk.at[t, pl.ds(c * size, count * rows), columns(h)]
        return remote(ref, ref, gather_send.at[t, c, h, 0], gather_recv.at[t, c, h],
                      (g, lax.rem(s + 1, LINE)))

    def part_copies(t, c, h):
        return [
            remote(part.at[t, c, h, some(lax.rem(s + k, LINE)), :], sent.at[t, c, h, k - 1],
                   part_send.at[t, c, h, k - 1], part_recv.at[t, c, h],
                   (g, lax.rem(s + k, LINE)))
            for k in range(1, LINE)
        ]

    def part_arrival(t, c, h):
        return remote(sent.at[t, c, h], sent.at[t, c, h], part_send.at[t, c, h, 0],
                      part_recv.at[t, c, h], (g, lax.rem(s + 1, LINE)))

    def final_copy(c, h):
        return remote(upd.at[TICKS - 1, c, h], final.at[pl.ds(c * rows, rows), columns(h)],
                      final_send.at[c, h], final_recv.at[c, h], (onward, s))

    load_items.wait()
    for c in range(CHUNKS):
        for h in range(HALVES):
            for copy in first_copies(c, h):
                copy.start()
        blk[0, chunk_rows(c, s), :] = items[c * rows : (c + 1) * rows, :]

    load_ratings.wait()
    for t in range(TICKS):
        for c in range(CHUNKS):
            for k in range(LINE):
                begin = t * BS + (k * CHUNKS + c) * rows
                targets[t, :, c * size + k * rows : c * size + (k + 1) * rows] = ratings[
                    :, begin : begin + rows
                ]
    load_users.wait()
    tall = min(256, n_users)

    def round_users(i, carry):
        at_rows = pl.ds(pl.multiple_of(i * tall, tall), tall)
        users_half[at_rows, :] = users[at_rows, :].astype(jnp.bfloat16)
        return carry

    lax.fori_loop(0, n_users // tall, round_users, 0)

    def work(t, c):
        ident = order_ref[0, lax.rem(g + n_blk - t % n_blk, n_blk)]
        column = lax.broadcasted_iota(jnp.int32, (1, size), 1)
        row_of = (column // rows) * (CHUNKS * rows) + c * rows + column % rows
        tile_of = row_of // (BS // tile_items)
        step_rows = 4 * tile_rows

        def product(at_rows, h):
            part_columns = slice(h * wide, (h + 1) * wide)
            return lax.dot_general(
                users_half[at_rows, part_columns],
                blk[t, c * size : (c + 1) * size, part_columns],
                (((1,), (1,)), ((), ())), preferred_element_type=jnp.float32,
            )

        for h in range(HALVES - 1):
            arrival(t, c, h).wait_recv()

            def add(i, carry):
                at_rows = pl.ds(pl.multiple_of(i * step_rows, step_rows), step_rows)
                if h == 0:
                    first_sum[at_rows, :] = product(at_rows, h)
                else:
                    first_sum[at_rows, :] += product(at_rows, h)
                return carry

            lax.fori_loop(0, n_users // step_rows, add, 0, unroll=True)
        arrival(t, c, HALVES - 1).wait_recv()

        def predict(i, carry):
            at_rows = pl.ds(pl.multiple_of(i * step_rows, step_rows), step_rows)
            predicted = (first_sum[at_rows, :] + product(at_rows, HALVES - 1)) * scale
            aims = targets[t, at_rows, c * size : (c + 1) * size].astype(jnp.float32)
            pieces = []
            for q in range(4):
                present = jnp.zeros((1, size), jnp.int32)
                for b in range(tile_items):
                    present = jnp.where(tile_of == b, presence_ref[i * 4 + q, b, ident], present)
                piece = slice(q * tile_rows, (q + 1) * tile_rows)
                pieces.append(present.astype(jnp.float32) * (predicted[piece] - aims[piece]))
            residual = jnp.concatenate(pieces, axis=0).astype(jnp.bfloat16)
            res[at_rows, c * size : (c + 1) * size] = residual
            res_t[:, at_rows] = residual.T
            return carry

        lax.fori_loop(0, n_users // step_rows, predict, 0, unroll=True)

        for h in range(HALVES):
            part[t, c, h] = (
                jnp.dot(res_t[...], users_half[:, h * wide : (h + 1) * wide],
                        preferred_element_type=jnp.float32)
                * scale
            ).astype(jnp.bfloat16)

            for copy in part_copies(t, c, h):
                copy.start()

    def renew(t, c):
        for h in range(HALVES):
            part_arrival(t, c, h).wait_recv()
            own = blk[t, chunk_rows(c, s), columns(h)].astype(jnp.float32)
            item_grad = part[t, c, h, some(s), :].astype(jnp.float32)
            for k in range(LINE - 1):
                item_grad = item_grad + sent[t, c, h, k].astype(jnp.float32)
            upd[t, c, h] = (own - step_items * (item_grad + decay_weight * own)).astype(
                jnp.bfloat16
            )
            if t < TICKS - 1:
                for copy in gather_copies(t, c, h):
                    copy.start()
            else:
                final_copy(c, h).start()

    def move_users(t):
        def body(i, carry):
            at_rows = pl.ds(pl.multiple_of(i * tall, tall), tall)
            for q in range(2):
                part_columns = slice(q * (R // 2), (q + 1) * (R // 2))
                user_grad = jnp.dot(
                    res[at_rows, :], blk[t, :, part_columns], preferred_element_type=jnp.float32
                ) * scale
                before = users[at_rows, part_columns]
                after = before - learn_users * (user_grad + decay_weight * before)
                users[at_rows, part_columns] = after
                if t < TICKS - 1:
                    users_half[at_rows, part_columns] = after.astype(jnp.bfloat16)
            return carry

        lax.fori_loop(0, n_users // tall, body, 0, unroll=2)

    for t in range(TICKS):
        work(t, 0)
        if t > 0:
            renew(t - 1, 1)
        work(t, 1)
        renew(t, 0)
        move_users(t)
    store_users = pltpu.make_async_copy(users, users_out, local_sem.at[1])
    store_users.start()
    renew(TICKS - 1, 1)

    for c in range(CHUNKS):
        for h in range(HALVES):
            final_copy(c, h).wait_recv()
    items_out[...] = final[...]
    for c in range(CHUNKS):
        for h in range(HALVES):
            for copy in first_copies(c, h):
                copy.wait_send()
            final_copy(c, h).wait_send()
            for t in range(TICKS):
                if t < TICKS - 1:
                    for copy in gather_copies(t, c, h):
                        copy.wait_send()

                for copy in part_copies(t, c, h):
                    copy.wait_send()
    store_users.wait()


def by_line(user_factors, item_factors, ratings, presence, visit_order):
    n_blk = lax.axis_size("blk")
    n_users = user_factors.shape[0]
    part_rows = item_factors.shape[0]
    rows = part_rows // CHUNKS
    size = rows * LINE
    wide = R // HALVES
    bf16, f32 = jnp.bfloat16, jnp.float32
    dma = pltpu.SemaphoreType.DMA
    vmem = pl.BlockSpec(memory_space=pltpu.VMEM)
    smem = pl.BlockSpec(memory_space=pltpu.SMEM)
    hbm = pl.BlockSpec(memory_space=pltpu.HBM)
    flops = 6 * TICKS * n_users * BS * R
    return pl.pallas_call(
        functools.partial(line_kernel, n_blk, step_size(LINE * n_users)),
        out_shape=(
            jax.ShapeDtypeStruct(user_factors.shape, f32),
            jax.ShapeDtypeStruct(item_factors.shape, bf16),
        ),
        in_specs=[hbm, hbm, hbm, smem, smem],
        out_specs=(hbm, vmem),
        scratch_shapes=[
            pltpu.VMEM((n_users, R), f32),
            pltpu.VMEM((part_rows, R), bf16),
            pltpu.VMEM((n_users, R), bf16),
            pltpu.VMEM(ratings.shape, bf16),
            pltpu.VMEM((TICKS, n_users, BS), bf16),
            pltpu.VMEM((n_users, BS), bf16),
            pltpu.VMEM((size, n_users), bf16),
            pltpu.VMEM((n_users, size), f32),
            pltpu.VMEM((TICKS, BS, R), bf16),
            pltpu.VMEM((TICKS, CHUNKS, HALVES, size, wide), bf16),
            pltpu.VMEM((TICKS, CHUNKS, HALVES, LINE - 1, rows, wide), bf16),
            pltpu.VMEM((TICKS, CHUNKS, HALVES, rows, wide), bf16),
            pltpu.VMEM((part_rows, R), bf16),
            dma((3,)),
            dma((TICKS, CHUNKS, HALVES, LINE)),
            dma((TICKS, CHUNKS, HALVES)),
            dma((TICKS, CHUNKS, HALVES, LINE - 1)),
            dma((TICKS, CHUNKS, HALVES)),
            dma((CHUNKS, HALVES)),
            dma((CHUNKS, HALVES)),
        ],
        compiler_params=pltpu.CompilerParams(
            collective_id=0, has_side_effects=True, vmem_limit_bytes=56 * 1024 * 1024
        ),
        cost_estimate=pl.CostEstimate(
            flops=flops, bytes_accessed=10 * n_users * R, transcendentals=0
        ),
    )(
        user_factors, item_factors, ratings,
        jnp.swapaxes(presence, 1, 2), visit_order.reshape(1, -1),
    )


def solution(mesh):
    in_specs = (
        P(("blk", "sub"), None),
        P(("blk", "sub"), None),
        P(("blk", "sub"), None),
        P(("blk", "sub"), None, None),
        P(),
    )
    out_specs = (P(("blk", "sub"), None), P(("blk", "sub"), None))
    lines = mesh.shape["sub"] == LINE and mesh.shape["blk"] > 2
    return jax.shard_map(
        by_line if lines else by_collectives,
        mesh=mesh, in_specs=in_specs, out_specs=out_specs, check_vma=False,
    )
```
